32 devices in a mesh: com: 8 (over z, x), arc: 4 (over y, core).
Axes of the slice: x: 2, y: 2, z: 4, core: 2. Of those that a mesh axis runs over, the one named last changes fastest.
Arguments:
- lfactor: float32 [16, 768, 768], P('com'), as said below
- links: float32 [16, 768, 4096], P('com', None, 'arc'), may hold values from -0.078125 to 0.078125
- usage: int32 [16, 4096], P('com', 'arc'), may hold values 0 or 1
- demands: bfloat16 [16, 768, 256], P('com'), may hold values from -6 to 6
- damping: float32 [4096], P('arc'), may hold values from 0.2 to 1
Outputs:
- schur: float32 [4096, 4096], P('com', 'arc')
- newton_y: float32 [4096, 256], P('arc')
- steps: float32 [16, 768, 256], P('com', None, 'arc')
The draws below stay inside these ranges and needn't reach their ends.
Inputs may be any that keep to these rules, and one draw needn't show every extreme that they name: lfactor[k] is lower triangular with its diagonal between 1 and 2.
All inputs are finite; a program needn't handle non-finite values. No bound on the sum of `usage` on one device may be relied on, other than what follows from the above.
Results may differ from the reference program's by a relative error of at most 0.003.
Values may be sent and summed in bfloat16 or wider, within the bound.
No kernel may reach another device: no remote copies, remote signals or barrier semaphores. Data moves between devices by JAX's collectives and lax.ppermute only.
A program may use at most 192 MiB of HBM per device.

```python
import math
import jax
import jax.numpy as jnp
from jax import lax

NODES = 768
ARCS = 4096
SCEN = 256
COMS = 16


def draw_lfactor(key, part):
    key_diag, key_off = jax.random.split(jax.random.fold_in(key, 11))
    diagonal = jnp.exp(jax.random.uniform(key_diag, (COMS, NODES), jnp.float32, 0.0, math.log(2.0)))
    spread = jax.random.normal(key_off, (COMS, NODES, NODES), jnp.float32) * (0.4 / math.sqrt(NODES))
    row_index = jnp.arange(NODES)[:, None]
    col_index = jnp.arange(NODES)[None, :]
    below = (row_index > col_index).astype(jnp.float32)
    on_diag = (row_index == col_index).astype(jnp.float32)
    return spread * below[None] + diagonal[:, :, None] * on_diag[None]


def plant(result, rng, least, high):
    spot = [jax.random.randint(jax.random.fold_in(rng, axis), (), 0, length) for axis, length in enumerate(result.shape)]
    widest = result.shape.index(max(result.shape))
    beside = spot[:widest] + [(spot[widest] + 1) % result.shape[widest]] + spot[widest + 1:]
    return result.at[tuple(spot)].set(least).at[tuple(beside)].set(high)


def spiked(values, stream_key, source, target, shards_of, factor):
    def block_of(dim):
        return (jnp.arange(values.shape[dim]) // (values.shape[dim] // shards_of)).reshape((-1,) + (1,) * (values.ndim - 1 - dim))

    one_side = jax.random.permutation(stream_key, shards_of)[block_of(target)]
    far = (block_of(target) + shards_of // 2) % shards_of
    return jnp.where((block_of(source) == one_side) | (block_of(source) == far), factor * values, values)


def level_of(rng, dims, cuts, low, high):
    def one(position, shards_of):
        draws = jax.random.uniform(jax.random.fold_in(jax.random.fold_in(rng, 6), position), (shards_of,), jnp.float32, low / len(cuts), high / len(cuts))
        return jnp.repeat(jnp.exp(draws), dims[position] // shards_of).reshape((-1,) + (1,) * (len(dims) - position - 1))

    gain = one(*cuts[0])
    for cut in cuts[1:]:
        gain = gain * one(*cut)
    return gain


def noise(stream_key, dims, width, limit, cuts=(), held_as=jnp.bfloat16):
    loudness = level_of(stream_key, dims, cuts, -0.22, 0.18) if cuts else 1.0
    entries = jax.random.normal(stream_key, dims, jnp.float32) * width * loudness
    return jnp.minimum(jnp.maximum(entries, -limit), limit).astype(held_as)


def bell_draw_with(rng, dims, deviation, reach, cuts, heavy, held_as=jnp.bfloat16):
    values = deviation * jax.random.normal(rng, dims, jnp.float32)
    if cuts:
        values = values * level_of(rng, dims, cuts, -0.22, 0.18)
    return jnp.clip(spiked(values, jax.random.fold_in(rng, 3), *heavy), -reach, reach).astype(held_as)


def setup_inputs(seed: int = 0) -> dict:
    key_of = jax.random.split(jax.random.key(seed), 6)
    return {
        "lfactor": draw_lfactor(jax.random.fold_in(key_of[5], 71), 0),
        "links": bell_draw_with(key_of[1], (COMS, NODES, ARCS), (COMS * NODES) ** -0.5, 0.078125, ((0, 8), (2, 4)), (0, 2, 8, 2.0), jnp.float32),
        "usage": plant((jax.random.randint(key_of[2], (COMS, ARCS), 0, 4) < 3).astype(jnp.int32), jax.random.fold_in(key_of[2], 1), 0, 1),
        "demands": noise(key_of[3], (COMS, NODES, SCEN), 1.0, 6.0, ((0, 8),)),
        "damping": jnp.clip(0.2 + 0.8 * jax.random.uniform(key_of[4], (ARCS,), jnp.float32) ** level_of(key_of[4], (ARCS,), ((0, 4),), -0.2, 0.2), 0.2, 1.0),
    }


def reference(lfactor, links, usage, demands, damping):
    coupling = links * usage[:, None, :].astype(jnp.float32)

    def forward_one(pair):
        factor, coupling_block = pair
        return jax.scipy.linalg.solve_triangular(factor, coupling_block, lower=True).astype(jnp.bfloat16)
    transformed = lax.map(forward_one, (lfactor, coupling))

    def accumulate(carry, items):
        panel_one, demand_one = items
        panel_wide = panel_one.astype(jnp.float32)
        demand_wide = demand_one.astype(jnp.float32)
        schur_sum = carry[0] + jnp.dot(panel_wide.T, panel_wide, precision=lax.Precision.HIGHEST)
        rhs_sum = carry[1] + jnp.dot(panel_wide.T, demand_wide, precision=lax.Precision.HIGHEST)
        return ((schur_sum, rhs_sum), None)
    start_carry = (jnp.zeros((ARCS, ARCS), jnp.float32), jnp.zeros((ARCS, SCEN), jnp.float32))
    (schur, rhs), _ = lax.scan(accumulate, start_carry, (transformed, demands))
    product = jnp.dot(schur, rhs, precision=lax.Precision.HIGHEST)
    newton_y = rhs - damping[:, None] * product
    rounded_y = newton_y.astype(jnp.bfloat16)

    def backward_one(triple):
        factor, panel_one, demand_one = triple
        correction = jnp.dot(panel_one.astype(jnp.float32), rounded_y.astype(jnp.float32), preferred_element_type=jnp.float32)
        return jax.scipy.linalg.solve_triangular(factor, demand_one.astype(jnp.float32) - correction, lower=True, trans=1)
    steps = lax.map(backward_one, (lfactor, transformed, demands))
    return (schur, newton_y, steps)
```

```python
import jax, jax.numpy as jnp
from jax import lax
from jax.experimental import pallas as pl
from jax.experimental.pallas import tpu as pltpu
from jax.sharding import PartitionSpec as P

BLOCK = 128
LEAF = 16

def halves(value):
    high = value.astype(jnp.bfloat16)
    low = (value - high.astype(jnp.float32)).astype(jnp.bfloat16)
    return high, low

def dot(a, b):
    return jnp.dot(a, b, preferred_element_type=jnp.float32)

def dot3(a, b):
    return dot(a[0], b[0]) + (dot(a[0], b[1]) + dot(a[1], b[0]))

def tdot(a, b):
    return lax.dot_general(a, b, (((0,), (0,)), ((), ())), preferred_element_type=jnp.float32)

def leaf_inverses(packed):
    rows, lanes = packed.shape
    lane = lax.broadcasted_iota(jnp.int32, (rows, lanes), 1)
    row = lax.broadcasted_iota(jnp.int32, (rows, lanes), 0) % LEAF
    inverse = (lane % LEAF == row).astype(jnp.float32)
    groups = rows // LEAF
    first = lane // LEAF * LEAF
    for step in range(LEAF):
        column = jnp.take_along_axis(packed, first + step, axis=1, mode="promise_in_bounds")
        def at_step(a):
            picked = a.reshape(groups, LEAF, lanes)[:, step : step + 1, :]
            return jnp.broadcast_to(picked, (groups, LEAF, lanes)).reshape(rows, lanes)
        done = at_step(inverse) / at_step(column)
        inverse = jnp.where(row > step, inverse - column * done, jnp.where(row == step, done, inverse))
    return inverse

def block_inverses(blocks):
    size = BLOCK
    lane = lax.broadcasted_iota(jnp.int32, (LEAF, size), 1)
    def pack(block):
        out = jnp.zeros((LEAF, size), jnp.float32)
        for part in range(size // LEAF):
            out = jnp.where(lane // LEAF == part, block[part * LEAF : (part + 1) * LEAF, :], out)
        return out
    leaves = leaf_inverses(jnp.concatenate([pack(b) for b in blocks], axis=0))
    inverses = []
    for index in range(len(blocks)):
        leaf = leaves[index * LEAF : (index + 1) * LEAF]
        inverses.append(jnp.concatenate(
            [jnp.where(lane // LEAF == part, leaf, 0.0) for part in range(size // LEAF)], axis=0))
    width = LEAF
    while width < size:
        parts = [(p, p + width) for p in range(width, size, 2 * width)]
        out = []
        for block, inverse in zip(blocks, inverses):
            odd = jnp.concatenate([inverse[p:q] for p, q in parts], axis=0)
            low = []
            for p, q in parts:
                spot = lax.broadcasted_iota(jnp.int32, (width, size), 1)
                low.append(jnp.where((spot >= p - width) & (spot < p), block[p:q], 0.0))
            low = jnp.concatenate([jnp.concatenate([jnp.zeros_like(l), l], axis=0) for l in low], axis=0)
            term = dot3(halves(odd), halves(low))
            term = dot3(halves(term), halves(inverse))
            pieces = []
            for number, (p, q) in enumerate(parts):
                pieces += [inverse[p - width : p], inverse[p:q] - term[number * width : (number + 1) * width]]
            out.append(jnp.concatenate(pieces, axis=0))
        inverses = out
        width *= 2
    return inverses

def forward_kernel(factor_ref, links_ref, usage_ref, demands_ref, out_ref, inverse_ref, rhs_ref, high_ref, low_ref):
    coms, nodes, _ = factor_ref.shape
    count = nodes // BLOCK
    span = lambda i: slice(i * BLOCK, (i + 1) * BLOCK)

    @pl.when(pl.program_id(0) == 0)
    def _():
        blocks = [factor_ref[c, span(i), span(i)] for c in range(coms) for i in range(count)]
        inverses = block_inverses(blocks)
        for c in range(coms):
            for i in range(count):
                inverse_ref[c, span(i)] = inverses[c * count + i]
            high, low = halves(factor_ref[c])
            high_ref[c] = high
            low_ref[c] = low

    solved = [[] for _ in range(coms)]
    for i in range(count):
        for c in range(coms):
            rest = links_ref[c, span(i)] * usage_ref[c].astype(jnp.float32)
            if i:
                high = jnp.concatenate([h for h, _ in solved[c]], axis=0)
                low = jnp.concatenate([l for _, l in solved[c]], axis=0)
                rest = rest - dot3((high_ref[c, span(i), : i * BLOCK], low_ref[c, span(i), : i * BLOCK]), (high, low))
            value = dot3(halves(inverse_ref[c, span(i)]), halves(rest))
            solved[c].append(halves(value))
            out_ref[c * nodes + i * BLOCK : c * nodes + (i + 1) * BLOCK] = solved[c][-1][0]
    rhs_ref[...] = sum(
        tdot(demands_ref[c], jnp.concatenate([h for h, _ in solved[c]], axis=0)) for c in range(coms))

def forward_solve(factor, links, usage, demands, tile=512):
    coms, nodes, arcs = links.shape
    scens = demands.shape[2]
    tile = min(tile, arcs)
    return pl.pallas_call(
        forward_kernel,
        grid=(arcs // tile,),
        in_specs=[
            pl.BlockSpec((coms, nodes, nodes), lambda t: (0, 0, 0)),
            pl.BlockSpec((coms, nodes, tile), lambda t: (0, 0, t)),
            pl.BlockSpec((coms, 1, tile), lambda t: (0, 0, t)),
            pl.BlockSpec((coms, nodes, scens), lambda t: (0, 0, 0)),
        ],
        out_specs=[
            pl.BlockSpec((coms * nodes, tile), lambda t: (0, t)),
            pl.BlockSpec((coms, nodes, BLOCK), lambda t: (0, 0, 0)),
            pl.BlockSpec((scens, tile), lambda t: (0, t)),
        ],
        out_shape=[
            jax.ShapeDtypeStruct((coms * nodes, arcs), jnp.bfloat16),
            jax.ShapeDtypeStruct((coms, nodes, BLOCK), jnp.float32),
            jax.ShapeDtypeStruct((scens, arcs), jnp.float32),
        ],
        scratch_shapes=[pltpu.VMEM((coms, nodes, nodes), jnp.bfloat16)] * 2,
        compiler_params=pltpu.CompilerParams(vmem_limit_bytes=48 * 2**20),
        cost_estimate=pl.CostEstimate(flops=6 * coms * nodes * nodes * arcs, bytes_accessed=4 * coms * nodes * (nodes + arcs) + 2 * coms * nodes * arcs, transcendentals=0),
    )(factor, links, usage.reshape(coms, 1, arcs), demands)

def backward_kernel(factor_ref, inverse_ref, demand_ref, correction_ref, out_ref):
    coms, nodes, _ = factor_ref.shape
    count = nodes // BLOCK
    span = lambda i: slice(i * BLOCK, (i + 1) * BLOCK)
    solved = [[] for _ in range(coms)]
    for i in reversed(range(count)):
        for c in range(coms):
            rest = demand_ref[c, span(i)].astype(jnp.float32).T - correction_ref[:, c * nodes + i * BLOCK : c * nodes + (i + 1) * BLOCK]
            if solved[c]:
                high = jnp.concatenate([h for h, _ in solved[c]], axis=1)
                low = jnp.concatenate([l for _, l in solved[c]], axis=1)
                rest = rest - dot3((high, low), halves(factor_ref[c, (i + 1) * BLOCK :, span(i)]))
            value = dot3(halves(rest), halves(inverse_ref[c, span(i)]))
            solved[c].insert(0, halves(value))
            out_ref[c, span(i)] = value.T

def backward_solve(factor, inverse, demand, correction):
    coms, nodes, scens = demand.shape
    return pl.pallas_call(
        backward_kernel,
        out_shape=jax.ShapeDtypeStruct((coms, nodes, scens), jnp.float32),
        compiler_params=pltpu.CompilerParams(vmem_limit_bytes=48 * 2**20),
    )(factor, inverse, demand, correction)

def times_kernel(*refs):
    *pieces, value_ref, out_ref = refs
    total = 0.0
    for number, piece in enumerate(pieces):
        total += lax.dot_general(value_ref[number], piece[...], (((1,), (1,)), ((), ())), preferred_element_type=jnp.float32)
    out_ref[...] = total

def project_kernel(*refs):
    *pieces, value_ref, out_ref = refs
    scens = value_ref.shape[0]
    both = jnp.concatenate(halves(value_ref[...]), axis=0)
    for number, piece in enumerate(pieces):
        found = dot(both, piece[...])
        out_ref[number] = found[:scens] + found[scens:]

def piece_call(kernel, pieces, value, shape):
    depth, columns = pieces[0].shape
    scens = value.shape[-2]
    return pl.pallas_call(
        kernel,
        out_shape=jax.ShapeDtypeStruct(shape, jnp.float32),
        compiler_params=pltpu.CompilerParams(vmem_limit_bytes=48 * 2**20),
        cost_estimate=pl.CostEstimate(flops=2 * len(pieces) * depth * columns * scens, bytes_accessed=2 * len(pieces) * depth * columns, transcendentals=0),
    )(*pieces, value)


def bit_count(size):
    return size.bit_length() - 1


def swap(value, axis, bits):
    size = lax.axis_size(axis)
    return lax.ppermute(value, axis, [(i, i ^ bits) for i in range(size)])


def pick(value, index, dim=0):
    return lax.dynamic_index_in_dim(value, index, dim, keepdims=False)


def wide(value):
    return value.astype(jnp.float32)


def after(value, *others):
    return lax.optimization_barrier((value, *others))[0]


class Link:

    def __init__(self, window=2):
        self.window = window
        self.results = []

    def send(self, values, axis, bits):
        if len(self.results) >= self.window:
            values = lax.optimization_barrier((tuple(values), self.results[-self.window]))[0]
        got = [swap(value, axis, bit) for value, bit in zip(values, bits)]
        self.results.append(got)
        return got


def on_device(lfactor, links, usage, demands, damping):
    place, arc = lax.axis_index("com"), lax.axis_index("arc")
    coms, arcs = lax.axis_size("com"), lax.axis_size("arc")
    side, outer, outers = place % 2, place // 2, coms // 2
    steps_out = range(1, outers)
    far_bits = [2 * step for step in steps_out]
    over_y, over_x, over_z = Link(), Link(), Link()

    def send_x(value):
        return over_x.send([value], "com", [1])[0]

    def send_z(values):
        return over_z.send(values, "com", far_bits)

    def send_y(values, bits):
        return over_y.send(values, "arc", bits)

    panel, inverse, local = forward_solve(lfactor, links, usage, demands)
    count, nodes, _ = lfactor.shape
    depth, width = panel.shape
    scens = demands.shape[2]
    share = scens // arcs
    chunks = arcs
    pairs = outers // chunks
    rows = width // coms
    span = pairs * rows
    halves_of = range(arcs // 2)

    def columns_of(value, which, chunk):
        starts = [((j * 2 + which) * chunks + chunk) * rows for j in range(pairs)]
        parts = [lax.dynamic_slice_in_dim(value, start, rows, value.ndim - 1) for start in starts]
        return jnp.concatenate(parts, axis=-1)

    own = [jnp.concatenate([columns_of(panel, 1 - side, n), columns_of(panel, side, n)], axis=1) for n in range(chunks)]
    lead, rest = {}, {}

    def split(chunk, half, first, second):
        lead[half, chunk] = jnp.concatenate([first[:, :span], second[:, :span]], axis=1)
        rest[half, chunk] = jnp.concatenate([first[:, span:], second[:, span:]], axis=1)

    def fetch_near(chunk):
        split(chunk, 0, own[chunk], swap(own[chunk], "arc", 1))

    def fetch_far(chunk):
        (got,) = send_y([own[chunk]], [2])
        split(chunk, 1, got, swap(got, "arc", 1))

    got_x = {}

    def schur_x(half, chunk):
        got_x[half, chunk] = send_x(tdot(lead[half, chunk], panel).astype(jnp.bfloat16))

    schur_out = [None] * chunks

    def schur_z(chunk):
        total = jnp.concatenate([tdot(rest[h, chunk], panel) + wide(got_x[h, chunk]) for h in halves_of])
        total = total.reshape(arcs, pairs, rows, width)
        def block_for(step):
            to = outer ^ step
            return pick(pick(total, arc ^ (to // pairs)), to % pairs)
        got = send_z([block_for(step).astype(jnp.bfloat16) for step in steps_out])
        schur_out[chunk] = sum((wide(g) for g in got), block_for(0))

    def reduce_outer(total):
        def part(owner):
            return lax.dynamic_slice_in_dim(pick(total, owner % chunks), owner // chunks * rows, rows, total.ndim - 2)
        got = send_z([part(outer ^ step) for step in steps_out])
        return sum(got, part(outer))

    def spread(value):
        held = jnp.stack([value] + send_z([value for _ in steps_out]))
        owners = [pick(held, outer ^ n) for n in range(outers)]
        near = jnp.stack([jnp.concatenate(owners[n::chunks], axis=-1) for n in range(chunks)])
        return send_x(near), near

    def paired(value):
        return jnp.stack([jnp.concatenate([value[n, 2 * h], value[n, 2 * h + 1]], axis=1) for h, n in rest])

    def times(far, near):
        found = piece_call(times_kernel, list(rest.values()), paired(near), (share, depth))
        return found + piece_call(times_kernel, [lead[k] for k in rest], paired(far), (share, depth))

    def project(pieces, inner):
        found = piece_call(project_kernel, list(pieces.values()), inner, (len(pieces), share, 2 * span))
        found = {k: found[n] for n, k in enumerate(pieces)}
        return jnp.stack([
            jnp.stack([found[h, n][:, p * span : (p + 1) * span] for h in halves_of for p in range(2)]) for n in range(chunks)])

    def of_side(which):
        return jnp.stack([columns_of(local, which, n) for n in range(chunks)])
    total = of_side(side) + send_x(of_side(1 - side))
    fetch_far(0)
    fetch_near(0)
    schur_x(0, 0)
    fetch_far(1)
    own_rhs = reduce_outer(total)
    fetch_near(1)
    schur_x(0, 1)
    slices = own_rhs.reshape(arcs, share, rows)
    others = range(1, arcs)
    rhs = jnp.stack([pick(slices, arc)] + [swap(pick(slices, arc ^ m), "arc", m) for m in others])
    own_damping = pick(pick(damping.reshape(pairs, 2, chunks, rows), side, 1).reshape(outers, rows), outer)
    damp = jnp.stack([own_damping] + [swap(own_damping, "arc", m) for m in others])
    fetch_far(2)
    schur_x(1, 0)
    fetch_near(2)
    fetch_near(3)
    fetch_far(3)
    inner = times(*spread(rhs.astype(jnp.bfloat16)))
    schur_x(0, 2)
    schur_z(0)
    schur_x(1, 1)
    schur_z(1)
    other = send_x(project(lead, inner))
    total = project(rest, inner) + other
    schur_x(0, 3)
    product = reduce_outer(total)
    schur_x(1, 2)
    schur_z(2)
    newton = rhs - damp[:, None, :] * product
    far_y, near_y = spread(newton.astype(jnp.bfloat16))
    schur_x(1, 3)
    schur_z(3)
    corrections = times(far_y, near_y)
    demand_share = lax.dynamic_slice_in_dim(demands, arc * share, share, 2)
    steps = backward_solve(lfactor, inverse, demand_share, corrections)

    def home(m):
        parts = [[jnp.where(side == which, near_y[n, m], far_y[n, m]) for n in range(chunks)] for which in range(2)]
        return jnp.concatenate([
            parts[which][n][:, j * rows : (j + 1) * rows]
            for j in range(pairs) for which in range(2) for n in range(chunks)], axis=1)
    held = jnp.stack([home(0)] + [swap(home(m), "arc", m) for m in others])
    newton_y = wide(jnp.concatenate([pick(held, arc ^ n) for n in range(arcs)])).T
    return (jnp.concatenate(schur_out, axis=0), newton_y, steps)


def solution(mesh):
    in_specs = (
        P("com", None, None),
        P("com", None, "arc"),
        P("com", "arc"),
        P("com", None, None),
        P("arc"),
    )
    out_specs = (P("com", "arc"), P("arc", None), P("com", None, "arc"))
    return jax.shard_map(
        on_device, mesh=mesh, in_specs=in_specs, out_specs=out_specs, check_vma=False
    )
```

```python
import jax, jax.numpy as jnp
from jax import lax
from jax.experimental import pallas as pl
from jax.experimental.pallas import tpu as pltpu
from jax.sharding import PartitionSpec as P

BLOCK = 128
LEAF = 16

def halves(value):
    high = value.astype(jnp.bfloat16)
    low = (value - high.astype(jnp.float32)).astype(jnp.bfloat16)
    return high, low

def dot(a, b):
    return jnp.dot(a, b, preferred_element_type=jnp.float32)

def dot3(a, b):
    return dot(a[0], b[0]) + (dot(a[0], b[1]) + dot(a[1], b[0]))

def tdot(a, b):
    return lax.dot_general(a, b, (((0,), (0,)), ((), ())), preferred_element_type=jnp.float32)

def leaf_inverses(packed):
    rows, lanes = packed.shape
    lane = lax.broadcasted_iota(jnp.int32, (rows, lanes), 1)
    row = lax.broadcasted_iota(jnp.int32, (rows, lanes), 0) % LEAF
    inverse = (lane % LEAF == row).astype(jnp.float32)
    groups = rows // LEAF
    first = lane // LEAF * LEAF
    for step in range(LEAF):
        column = jnp.take_along_axis(packed, first + step, axis=1, mode="promise_in_bounds")
        def at_step(a):
            picked = a.reshape(groups, LEAF, lanes)[:, step : step + 1, :]
            return jnp.broadcast_to(picked, (groups, LEAF, lanes)).reshape(rows, lanes)
        done = at_step(inverse) / at_step(column)
        inverse = jnp.where(row > step, inverse - column * done, jnp.where(row == step, done, inverse))
    return inverse

def block_inverses(blocks):
    size = BLOCK
    lane = lax.broadcasted_iota(jnp.int32, (LEAF, size), 1)
    def pack(block):
        out = jnp.zeros((LEAF, size), jnp.float32)
        for part in range(size // LEAF):
            out = jnp.where(lane // LEAF == part, block[part * LEAF : (part + 1) * LEAF, :], out)
        return out
    leaves = leaf_inverses(jnp.concatenate([pack(b) for b in blocks], axis=0))
    inverses = []
    for index in range(len(blocks)):
        leaf = leaves[index * LEAF : (index + 1) * LEAF]
        inverses.append(jnp.concatenate(
            [jnp.where(lane // LEAF == part, leaf, 0.0) for part in range(size // LEAF)], axis=0))
    width = LEAF
    while width < size:
        parts = [(p, p + width) for p in range(width, size, 2 * width)]
        out = []
        for block, inverse in zip(blocks, inverses):
            odd = jnp.concatenate([inverse[p:q] for p, q in parts], axis=0)
            low = []
            for p, q in parts:
                spot = lax.broadcasted_iota(jnp.int32, (width, size), 1)
                low.append(jnp.where((spot >= p - width) & (spot < p), block[p:q], 0.0))
            low = jnp.concatenate([jnp.concatenate([jnp.zeros_like(l), l], axis=0) for l in low], axis=0)
            term = dot3(halves(odd), halves(low))
            term = dot3(halves(term), halves(inverse))
            pieces = []
            for number, (p, q) in enumerate(parts):
                pieces += [inverse[p - width : p], inverse[p:q] - term[number * width : (number + 1) * width]]
            out.append(jnp.concatenate(pieces, axis=0))
        inverses = out
        width *= 2
    return inverses

def forward_kernel(factor_ref, links_ref, usage_ref, demands_ref, out_ref, inverse_ref, rhs_ref, high_ref, low_ref):
    coms, nodes, _ = factor_ref.shape
    count = nodes // BLOCK
    span = lambda i: slice(i * BLOCK, (i + 1) * BLOCK)

    @pl.when(pl.program_id(0) == 0)
    def _():
        blocks = [factor_ref[c, span(i), span(i)] for c in range(coms) for i in range(count)]
        inverses = block_inverses(blocks)
        for c in range(coms):
            for i in range(count):
                inverse_ref[c, span(i)] = inverses[c * count + i]
            high, low = halves(factor_ref[c])
            high_ref[c] = high
            low_ref[c] = low

    solved = [[] for _ in range(coms)]
    for i in range(count):
        for c in range(coms):
            rest = links_ref[c, span(i)] * usage_ref[c].astype(jnp.float32)
            if i:
                high = jnp.concatenate([h for h, _ in solved[c]], axis=0)
                low = jnp.concatenate([l for _, l in solved[c]], axis=0)
                rest = rest - dot3((high_ref[c, span(i), : i * BLOCK], low_ref[c, span(i), : i * BLOCK]), (high, low))
            value = dot3(halves(inverse_ref[c, span(i)]), halves(rest))
            solved[c].append(halves(value))
            out_ref[c * nodes + i * BLOCK : c * nodes + (i + 1) * BLOCK] = solved[c][-1][0]
    rhs_ref[...] = sum(
        tdot(demands_ref[c], jnp.concatenate([h for h, _ in solved[c]], axis=0)) for c in range(coms))

def forward_solve(factor, links, usage, demands, tile=512):
    coms, nodes, arcs = links.shape
    scens = demands.shape[2]
    tile = min(tile, arcs)
    return pl.pallas_call(
        forward_kernel,
        grid=(arcs // tile,),
        in_specs=[
            pl.BlockSpec((coms, nodes, nodes), lambda t: (0, 0, 0)),
            pl.BlockSpec((coms, nodes, tile), lambda t: (0, 0, t)),
            pl.BlockSpec((coms, 1, tile), lambda t: (0, 0, t)),
            pl.BlockSpec((coms, nodes, scens), lambda t: (0, 0, 0)),
        ],
        out_specs=[
            pl.BlockSpec((coms * nodes, tile), lambda t: (0, t)),
            pl.BlockSpec((coms, nodes, BLOCK), lambda t: (0, 0, 0)),
            pl.BlockSpec((scens, tile), lambda t: (0, t)),
        ],
        out_shape=[
            jax.ShapeDtypeStruct((coms * nodes, arcs), jnp.bfloat16),
            jax.ShapeDtypeStruct((coms, nodes, BLOCK), jnp.float32),
            jax.ShapeDtypeStruct((scens, arcs), jnp.float32),
        ],
        scratch_shapes=[pltpu.VMEM((coms, nodes, nodes), jnp.bfloat16)] * 2,
        compiler_params=pltpu.CompilerParams(vmem_limit_bytes=48 * 2**20),
        cost_estimate=pl.CostEstimate(flops=6 * coms * nodes * nodes * arcs, bytes_accessed=4 * coms * nodes * (nodes + arcs) + 2 * coms * nodes * arcs, transcendentals=0),
    )(factor, links, usage.reshape(coms, 1, arcs), demands)

def backward_kernel(factor_ref, inverse_ref, demand_ref, correction_ref, out_ref):
    coms, nodes, _ = factor_ref.shape
    count = nodes // BLOCK
    span = lambda i: slice(i * BLOCK, (i + 1) * BLOCK)
    solved = [[] for _ in range(coms)]
    for i in reversed(range(count)):
        for c in range(coms):
            rest = demand_ref[c, span(i)].astype(jnp.float32).T - correction_ref[:, c * nodes + i * BLOCK : c * nodes + (i + 1) * BLOCK]
            if solved[c]:
                high = jnp.concatenate([h for h, _ in solved[c]], axis=1)
                low = jnp.concatenate([l for _, l in solved[c]], axis=1)
                rest = rest - dot3((high, low), halves(factor_ref[c, (i + 1) * BLOCK :, span(i)]))
            value = dot3(halves(rest), halves(inverse_ref[c, span(i)]))
            solved[c].insert(0, halves(value))
            out_ref[c, span(i)] = value.T

def backward_solve(factor, inverse, demand, correction):
    coms, nodes, scens = demand.shape
    return pl.pallas_call(
        backward_kernel,
        out_shape=jax.ShapeDtypeStruct((coms, nodes, scens), jnp.float32),
        compiler_params=pltpu.CompilerParams(vmem_limit_bytes=48 * 2**20),
    )(factor, inverse, demand, correction)

def times_kernel(*refs):
    *pieces, value_ref, out_ref = refs
    total = 0.0
    for number, piece in enumerate(pieces):
        total += lax.dot_general(value_ref[number], piece[...], (((1,), (1,)), ((), ())), preferred_element_type=jnp.float32)
    out_ref[...] = total

def project_kernel(*refs):
    *pieces, value_ref, out_ref = refs
    scens = value_ref.shape[0]
    both = jnp.concatenate(halves(value_ref[...]), axis=0)
    for number, piece in enumerate(pieces):
        found = dot(both, piece[...])
        out_ref[number] = found[:scens] + found[scens:]

def piece_call(kernel, pieces, value, shape):
    depth, columns = pieces[0].shape
    scens = value.shape[-2]
    return pl.pallas_call(
        kernel,
        out_shape=jax.ShapeDtypeStruct(shape, jnp.float32),
        compiler_params=pltpu.CompilerParams(vmem_limit_bytes=48 * 2**20),
        cost_estimate=pl.CostEstimate(flops=2 * len(pieces) * depth * columns * scens, bytes_accessed=2 * len(pieces) * depth * columns, transcendentals=0),
    )(*pieces, value)


def bit_count(size):
    return size.bit_length() - 1


def swap(value, axis, bits):
    size = lax.axis_size(axis)
    return lax.ppermute(value, axis, [(i, i ^ bits) for i in range(size)])


def pick(value, index, dim=0):
    return lax.dynamic_index_in_dim(value, index, dim, keepdims=False)


def wide(value):
    return value.astype(jnp.float32)


def together(*values):
    return lax.optimization_barrier(values)


def on_device(lfactor, links, usage, demands, damping):
    place, arc = lax.axis_index("com"), lax.axis_index("arc")
    coms, arcs = lax.axis_size("com"), lax.axis_size("arc")
    side, outer, outers = place % 2, place // 2, coms // 2
    steps_out = range(1, outers)
    far_bits = [2 * step for step in steps_out]

    def send_x(value):
        return swap(value, "com", 1)

    def send_z(values):
        return [swap(value, "com", bits) for value, bits in zip(values, far_bits)]

    panel, inverse, local = forward_solve(lfactor, links, usage, demands)
    count, nodes, _ = lfactor.shape
    depth, width = panel.shape
    scens = demands.shape[2]
    share = scens // arcs
    chunks = arcs
    pairs = outers // chunks
    rows = width // coms
    span = pairs * rows
    halves_of = range(arcs // 2)

    def columns_of(value, which, chunk):
        starts = [((j * 2 + which) * chunks + chunk) * rows for j in range(pairs)]
        parts = [lax.dynamic_slice_in_dim(value, start, rows, value.ndim - 1) for start in starts]
        return jnp.concatenate(parts, axis=-1)

    own = [jnp.concatenate([columns_of(panel, 1 - side, n), columns_of(panel, side, n)], axis=1) for n in range(chunks)]
    lead, rest = {}, {}

    def split(chunk, half, first):
        second = swap(first, "arc", 1)
        lead[half, chunk] = jnp.concatenate([first[:, :span], second[:, :span]], axis=1)
        rest[half, chunk] = jnp.concatenate([first[:, span:], second[:, span:]], axis=1)

    def lead_rows(half, chunk):
        return tdot(lead[half, chunk], panel).astype(jnp.bfloat16)

    def schur_parts(chunk, got):
        total = jnp.concatenate([tdot(rest[h, chunk], panel) + wide(got[h]) for h in halves_of])
        total = total.reshape(arcs, pairs, rows, width)
        def block_for(step):
            to = outer ^ step
            return pick(pick(total, arc ^ (to // pairs)), to % pairs)
        return block_for(0), [block_for(step).astype(jnp.bfloat16) for step in steps_out]

    def add_all(kept, got):
        return sum((wide(g) for g in got), kept)

    def outer_parts(total):
        def part(owner):
            return lax.dynamic_slice_in_dim(pick(total, owner % chunks), owner // chunks * rows, rows, total.ndim - 2)
        return part(outer), [part(outer ^ step) for step in steps_out]

    def gather_outer(value):
        held = jnp.stack([value] + send_z([value for _ in steps_out]))
        owners = [pick(held, outer ^ n) for n in range(outers)]
        return jnp.stack([jnp.concatenate(owners[n::chunks], axis=-1) for n in range(chunks)])

    def paired(value):
        return jnp.stack([jnp.concatenate([value[n, 2 * h], value[n, 2 * h + 1]], axis=1) for h, n in rest])

    def times(far, near):
        found = piece_call(times_kernel, list(rest.values()), paired(near), (share, depth))
        return found + piece_call(times_kernel, [lead[k] for k in rest], paired(far), (share, depth))

    def project(pieces, inner):
        found = piece_call(project_kernel, list(pieces.values()), inner, (len(pieces), share, 2 * span))
        found = {k: found[n] for n, k in enumerate(pieces)}
        return jnp.stack([
            jnp.stack([found[h, n][:, p * span : (p + 1) * span] for h in halves_of for p in range(2)]) for n in range(chunks)])

    def of_side(which):
        return jnp.stack([columns_of(local, which, n) for n in range(chunks)])
    others = range(1, arcs)
    own_damping = pick(pick(damping.reshape(pairs, 2, chunks, rows), side, 1).reshape(outers, rows), outer)
    damp = jnp.stack([own_damping] + [swap(own_damping, "arc", m) for m in others])

    got = send_x(of_side(1 - side))
    far0 = swap(own[0], "arc", 2)
    split(0, 0, own[0])
    total = of_side(side) + got
    total, x00, own[1] = together(total, lead_rows(0, 0), own[1])
    kept, sent = outer_parts(total)
    got = send_z(sent)
    x00 = send_x(x00)
    far1 = swap(own[1], "arc", 2)
    split(0, 1, far0)
    split(1, 0, own[1])
    own_rhs = add_all(kept, got)
    own_rhs, x00, x10, x01 = together(own_rhs, x00, lead_rows(1, 0), lead_rows(0, 1))
    slices = own_rhs.reshape(arcs, share, rows)
    rhs = jnp.stack([pick(slices, arc)] + [swap(pick(slices, arc ^ m), "arc", m) for m in others])
    x10, x01 = send_x(x10), send_x(x01)
    rhs, own[2], own[3] = together(rhs, own[2], own[3])
    far2, far3 = swap(own[2], "arc", 2), swap(own[3], "arc", 2)
    split(1, 1, far1)
    near = gather_outer(rhs.astype(jnp.bfloat16))
    kept0, sent0 = schur_parts(0, [x00, x10])
    near, sent0, x01, x11 = together(near, sent0, x01, lead_rows(1, 1))
    far = send_x(near)
    z0 = send_z(sent0)
    x11 = send_x(x11)
    split(2, 0, own[2])
    split(2, 1, far2)
    kept1, sent1 = schur_parts(1, [x01, x11])
    far, z0, sent1, x02, x12 = together(far, z0, sent1, lead_rows(0, 2), lead_rows(1, 2))
    z1 = send_z(sent1)
    x02, x12 = send_x(x02), send_x(x12)
    split(3, 0, own[3])
    split(3, 1, far3)
    inner = times(far, near)
    kept2, sent2 = schur_parts(2, [x02, x12])
    sent, z1, sent2, x03 = together(project(lead, inner), z1, sent2, lead_rows(0, 3))
    got = send_x(sent)
    z2 = send_z(sent2)
    x03 = send_x(x03)
    total = project(rest, inner) + got
    total, z2, x03, x13 = together(total, z2, x03, lead_rows(1, 3))
    kept, sent = outer_parts(total)
    got = send_z(sent)
    x13 = send_x(x13)
    newton = rhs - damp[:, None, :] * add_all(kept, got)
    kept3, sent3 = schur_parts(3, [x03, x13])
    newton, sent3 = together(newton.astype(jnp.bfloat16), sent3)
    near_y = gather_outer(newton)
    z3 = send_z(sent3)
    far_y = send_x(near_y)
    corrections = times(far_y, near_y)
    demand_share = lax.dynamic_slice_in_dim(demands, arc * share, share, 2)
    steps = backward_solve(lfactor, inverse, demand_share, corrections)
    schur_out = [add_all(kept, got) for kept, got in [(kept0, z0), (kept1, z1), (kept2, z2), (kept3, z3)]]

    def home(m):
        parts = [[jnp.where(side == which, near_y[n, m], far_y[n, m]) for n in range(chunks)] for which in range(2)]
        return jnp.concatenate([
            parts[which][n][:, j * rows : (j + 1) * rows]
            for j in range(pairs) for which in range(2) for n in range(chunks)], axis=1)
    held = jnp.stack([home(0)] + [swap(home(m), "arc", m) for m in others])
    newton_y = wide(jnp.concatenate([pick(held, arc ^ n) for n in range(arcs)])).T
    return (jnp.concatenate(schur_out, axis=0), newton_y, steps)


def solution(mesh):
    in_specs = (
        P("com", None, None),
        P("com", None, "arc"),
        P("com", "arc"),
        P("com", None, None),
        P("arc"),
    )
    out_specs = (P("com", "arc"), P("arc", None), P("com", None, "arc"))
    return jax.shard_map(
        on_device, mesh=mesh, in_specs=in_specs, out_specs=out_specs, check_vma=False
    )
```

```python
import functools
import jax, jax.numpy as jnp
from jax import lax
from jax.experimental import pallas as pl
from jax.experimental.pallas import tpu as pltpu
from jax.sharding import PartitionSpec as P

BLOCK = 128
LEAF = 16

def halves(value):
    high = value.astype(jnp.bfloat16)
    low = (value - high.astype(jnp.float32)).astype(jnp.bfloat16)
    return high, low

def dot(a, b):
    return jnp.dot(a, b, preferred_element_type=jnp.float32)

def dot3(a, b):
    return dot(a[0], b[0]) + (dot(a[0], b[1]) + dot(a[1], b[0]))

def tdot(a, b):
    return lax.dot_general(a, b, (((0,), (0,)), ((), ())), preferred_element_type=jnp.float32)

def leaf_inverses(packed):
    rows, lanes = packed.shape
    lane = lax.broadcasted_iota(jnp.int32, (rows, lanes), 1)
    row = lax.broadcasted_iota(jnp.int32, (rows, lanes), 0) % LEAF
    inverse = (lane % LEAF == row).astype(jnp.float32)
    groups = rows // LEAF
    first = lane // LEAF * LEAF
    for step in range(LEAF):
        column = jnp.take_along_axis(packed, first + step, axis=1, mode="promise_in_bounds")
        def at_step(a):
            picked = a.reshape(groups, LEAF, lanes)[:, step : step + 1, :]
            return jnp.broadcast_to(picked, (groups, LEAF, lanes)).reshape(rows, lanes)
        done = at_step(inverse) / at_step(column)
        inverse = jnp.where(row > step, inverse - column * done, jnp.where(row == step, done, inverse))
    return inverse

def block_inverses(blocks):
    size = BLOCK
    lane = lax.broadcasted_iota(jnp.int32, (LEAF, size), 1)
    def pack(block):
        out = jnp.zeros((LEAF, size), jnp.float32)
        for part in range(size // LEAF):
            out = jnp.where(lane // LEAF == part, block[part * LEAF : (part + 1) * LEAF, :], out)
        return out
    leaves = leaf_inverses(jnp.concatenate([pack(b) for b in blocks], axis=0))
    inverses = []
    for index in range(len(blocks)):
        leaf = leaves[index * LEAF : (index + 1) * LEAF]
        inverses.append(jnp.concatenate(
            [jnp.where(lane // LEAF == part, leaf, 0.0) for part in range(size // LEAF)], axis=0))
    width = LEAF
    while width < size:
        parts = [(p, p + width) for p in range(width, size, 2 * width)]
        out = []
        for block, inverse in zip(blocks, inverses):
            odd = jnp.concatenate([inverse[p:q] for p, q in parts], axis=0)
            low = []
            for p, q in parts:
                spot = lax.broadcasted_iota(jnp.int32, (width, size), 1)
                low.append(jnp.where((spot >= p - width) & (spot < p), block[p:q], 0.0))
            low = jnp.concatenate([jnp.concatenate([jnp.zeros_like(l), l], axis=0) for l in low], axis=0)
            term = dot3(halves(odd), halves(low))
            term = dot3(halves(term), halves(inverse))
            pieces = []
            for number, (p, q) in enumerate(parts):
                pieces += [inverse[p - width : p], inverse[p:q] - term[number * width : (number + 1) * width]]
            out.append(jnp.concatenate(pieces, axis=0))
        inverses = out
        width *= 2
    return inverses

def forward_kernel(side_ref, factor_ref, links_ref, usage_ref, demands_ref, out_ref, inverse_ref, rhs_ref, *others):
    *own_refs, high_ref, low_ref = others
    coms, nodes, _ = factor_ref.shape
    count = nodes // BLOCK
    span = lambda i: slice(i * BLOCK, (i + 1) * BLOCK)

    @pl.when(pl.program_id(0) == 0)
    def _():
        blocks = [factor_ref[c, span(i), span(i)] for c in range(coms) for i in range(count)]
        inverses = block_inverses(blocks)
        for c in range(coms):
            for i in range(count):
                inverse_ref[c, span(i)] = inverses[c * count + i]
            high, low = halves(factor_ref[c])
            high_ref[c] = high
            low_ref[c] = low

    solved = [[] for _ in range(coms)]
    for i in range(count):
        for c in range(coms):
            rest = links_ref[c, span(i)] * usage_ref[c].astype(jnp.float32)
            if i:
                high = jnp.concatenate([h for h, _ in solved[c]], axis=0)
                low = jnp.concatenate([l for _, l in solved[c]], axis=0)
                rest = rest - dot3((high_ref[c, span(i), : i * BLOCK], low_ref[c, span(i), : i * BLOCK]), (high, low))
            value = dot3(halves(inverse_ref[c, span(i)]), halves(rest))
            solved[c].append(halves(value))
            out_ref[c * nodes + i * BLOCK : c * nodes + (i + 1) * BLOCK] = solved[c][-1][0]
    found = jnp.concatenate([h for c in range(coms) for h, _ in solved[c]], axis=0)
    rhs_ref[...] = tdot(demands_ref[...].reshape(coms * nodes, -1), found)
    if own_refs:
        width = found.shape[1] // len(own_refs)
        spot = pl.ds(pl.multiple_of(jnp.where(pl.program_id(0) == side_ref[0], width, 0), width), width)
        for number, own_ref in enumerate(own_refs):
            own_ref[:, spot] = found[:, number * width : (number + 1) * width]

def forward_solve(factor, links, usage, demands, side, chunks):
    coms, nodes, arcs = links.shape
    scens = demands.shape[2]
    tile = arcs // 2
    span = tile // chunks if chunks else 0
    depth = coms * nodes
    once = lambda *shape: pl.BlockSpec(shape, lambda t, _: (0,) * len(shape))
    return pl.pallas_call(
        forward_kernel,
        grid_spec=pltpu.PrefetchScalarGridSpec(
            num_scalar_prefetch=1,
            grid=(arcs // tile,),
            in_specs=[
                once(coms, nodes, nodes),
                pl.BlockSpec((coms, nodes, tile), lambda t, _: (0, 0, t)),
                pl.BlockSpec((coms, 1, tile), lambda t, _: (0, 0, t)),
                once(coms, nodes, scens),
            ],
            out_specs=[
                pl.BlockSpec((depth, tile), lambda t, _: (0, t)),
                once(coms, nodes, BLOCK),
                pl.BlockSpec((scens, tile), lambda t, _: (0, t)),
            ] + [once(depth, 2 * span)] * chunks,
            scratch_shapes=[pltpu.VMEM((coms, nodes, nodes), jnp.bfloat16)] * 2,
        ),
        out_shape=[
            jax.ShapeDtypeStruct((depth, arcs), jnp.bfloat16),
            jax.ShapeDtypeStruct((coms, nodes, BLOCK), jnp.float32),
            jax.ShapeDtypeStruct((scens, arcs), jnp.float32),
        ] + [jax.ShapeDtypeStruct((depth, 2 * span), jnp.bfloat16)] * chunks,
        compiler_params=pltpu.CompilerParams(vmem_limit_bytes=48 * 2**20),
        cost_estimate=pl.CostEstimate(
            flops=6 * coms * nodes * nodes * arcs,
            bytes_accessed=4 * coms * nodes * (nodes + arcs) + 2 * coms * nodes * arcs, transcendentals=0),
    )(side.reshape(1), factor, links, usage.reshape(coms, 1, arcs), demands)


def backward_kernel(factor_ref, inverse_ref, demand_ref, correction_ref, out_ref):
    coms, nodes, _ = factor_ref.shape
    count = nodes // BLOCK
    span = lambda i: slice(i * BLOCK, (i + 1) * BLOCK)
    solved = [[] for _ in range(coms)]
    for i in reversed(range(count)):
        for c in range(coms):
            rest = demand_ref[c, span(i)].astype(jnp.float32).T - correction_ref[:, c * nodes + i * BLOCK : c * nodes + (i + 1) * BLOCK]
            if solved[c]:
                high = jnp.concatenate([h for h, _ in solved[c]], axis=1)
                low = jnp.concatenate([l for _, l in solved[c]], axis=1)
                rest = rest - dot3((high, low), halves(factor_ref[c, (i + 1) * BLOCK :, span(i)]))
            value = dot3(halves(rest), halves(inverse_ref[c, span(i)]))
            solved[c].insert(0, halves(value))
            out_ref[c, span(i)] = value.T

def multiply(pieces, value_ref):
    total = 0.0
    for (half, chunk), piece in pieces.items():
        value = jnp.concatenate([value_ref[chunk, 2 * half], value_ref[chunk, 2 * half + 1]], axis=1)
        total += lax.dot_general(value, piece[...], (((1,), (1,)), ((), ())), preferred_element_type=jnp.float32)
    return total


def inner_kernel(keys, *refs):
    count = len(keys)
    lead, rest = dict(zip(keys, refs[:count])), dict(zip(keys, refs[count : 2 * count]))
    far_ref, near_ref, lead_out, rest_out = refs[2 * count :]
    found = multiply(lead, far_ref) + multiply(rest, near_ref)
    scens = found.shape[0]
    both = jnp.concatenate(halves(found), axis=0)
    for pieces, out in ((lead, lead_out), (rest, rest_out)):
        for (half, chunk), piece in pieces.items():
            product = dot(both, piece[...])
            product = product[:scens] + product[scens:]
            span = product.shape[1] // 2
            out[chunk, 2 * half] = product[:, :span]
            out[chunk, 2 * half + 1] = product[:, span:]


def piece_cost(lead, times):
    pieces = len(lead) * 2
    depth, columns = next(iter(lead.values())).shape
    return dict(flops=2 * times * pieces * depth * columns * 64, bytes_accessed=2 * pieces * depth * columns, transcendentals=0)


def through_columns(lead, rest, far, near):
    keys = tuple(lead)
    shape = jax.ShapeDtypeStruct(far.shape, jnp.float32)
    return pl.pallas_call(
        functools.partial(inner_kernel, keys),
        out_shape=[shape, shape],
        compiler_params=pltpu.CompilerParams(vmem_limit_bytes=48 * 2**20),
        cost_estimate=pl.CostEstimate(**piece_cost(lead, 2)),
    )(*[lead[k] for k in keys], *[rest[k] for k in keys], far, near)


def steps_kernel(keys, *refs):
    count = len(keys)
    lead, rest = dict(zip(keys, refs[:count])), dict(zip(keys, refs[count : 2 * count]))
    far_ref, near_ref, factor_ref, inverse_ref, demand_ref, out_ref, correction_ref = refs[2 * count :]
    correction_ref[...] = multiply(rest, near_ref) + multiply(lead, far_ref)
    backward_kernel(factor_ref, inverse_ref, demand_ref, correction_ref, out_ref)


def corrected_steps(lead, rest, far, near, factor, inverse, demand):
    keys = tuple(lead)
    coms, nodes, scens = demand.shape
    return pl.pallas_call(
        functools.partial(steps_kernel, keys),
        out_shape=jax.ShapeDtypeStruct(demand.shape, jnp.float32),
        scratch_shapes=[pltpu.VMEM((scens, coms * nodes), jnp.float32)],
        compiler_params=pltpu.CompilerParams(vmem_limit_bytes=48 * 2**20),
        cost_estimate=pl.CostEstimate(**piece_cost(lead, 1)),
    )(*[lead[k] for k in keys], *[rest[k] for k in keys], far, near, factor, inverse, demand)


def bit_count(size):
    return size.bit_length() - 1


def swap(value, axis, bits):
    size = lax.axis_size(axis)
    return lax.ppermute(value, axis, [(i, i ^ bits) for i in range(size)])


def pick(value, index, dim=0):
    return lax.dynamic_index_in_dim(value, index, dim, keepdims=False)


def wide(value):
    return value.astype(jnp.float32)


def together(*values):
    return lax.optimization_barrier(values)


def on_device(lfactor, links, usage, demands, damping):
    place, arc = lax.axis_index("com"), lax.axis_index("arc")
    coms, arcs = lax.axis_size("com"), lax.axis_size("arc")
    side, outer, outers = place % 2, place // 2, coms // 2
    steps_out = range(1, outers)
    far_bits = [2 * step for step in steps_out]

    def send_x(value):
        return swap(value, "com", 1)

    def send_z(values):
        return [swap(value, "com", bits) for value, bits in zip(values, far_bits)]

    count, nodes, width = links.shape
    depth = count * nodes
    scens = demands.shape[2]
    share = scens // arcs
    chunks = arcs
    pairs = outers // chunks
    rows = width // coms
    span = pairs * rows
    direct = pairs == 1 and rows % 128 == 0
    panel, inverse, local, *own = forward_solve(lfactor, links, usage, demands, side, chunks if direct else 0)
    halves_of = range(arcs // 2)

    def columns_of(value, which, chunk):
        starts = [((j * 2 + which) * chunks + chunk) * rows for j in range(pairs)]
        parts = [lax.dynamic_slice_in_dim(value, start, rows, value.ndim - 1) for start in starts]
        return jnp.concatenate(parts, axis=-1)

    if not direct:
        own = [jnp.concatenate([columns_of(panel, 1 - side, n), columns_of(panel, side, n)], axis=1) for n in range(chunks)]
    lead, rest = {}, {}

    def split(chunk, half, first):
        second = swap(first, "arc", 1)
        lead[half, chunk] = jnp.concatenate([first[:, :span], second[:, :span]], axis=1)
        rest[half, chunk] = jnp.concatenate([first[:, span:], second[:, span:]], axis=1)

    def lead_rows(half, chunk):
        return tdot(lead[half, chunk], panel).astype(jnp.bfloat16)

    def schur_parts(chunk, got):
        total = jnp.concatenate([tdot(rest[h, chunk], panel) + wide(got[h]) for h in halves_of])
        total = total.reshape(arcs, pairs, rows, width)
        def block_for(step):
            to = outer ^ step
            return pick(pick(total, arc ^ (to // pairs)), to % pairs)
        return block_for(0), [block_for(step).astype(jnp.bfloat16) for step in steps_out]

    def add_all(kept, got):
        return sum((wide(g) for g in got), kept)

    def outer_parts(total):
        def part(owner):
            return lax.dynamic_slice_in_dim(pick(total, owner % chunks), owner // chunks * rows, rows, total.ndim - 2)
        return part(outer), [part(outer ^ step) for step in steps_out]

    def in_chunks(value, got):
        held = jnp.stack([value] + got)
        owners = [pick(held, outer ^ n) for n in range(outers)]
        return jnp.stack([jnp.concatenate(owners[n::chunks], axis=-1) for n in range(chunks)])

    def of_side(which):
        return jnp.stack([columns_of(local, which, n) for n in range(chunks)])
    others = range(1, arcs)
    got = send_x(of_side(1 - side))
    far0 = swap(own[0], "arc", 2)
    split(0, 0, own[0])
    split(1, 0, own[1])
    total = of_side(side) + got
    total, x00, own[1] = together(total, lead_rows(0, 0), own[1])
    kept, sent = outer_parts(total)
    far1 = swap(own[1], "arc", 2)
    got = send_z(sent)
    x00 = send_x(x00)
    split(0, 1, far0)
    own_rhs = add_all(kept, got)
    own_rhs, x00, x10 = together(own_rhs, x00, lead_rows(1, 0))
    slices = own_rhs.reshape(arcs, share, rows)
    sent = [pick(slices, arc ^ m) for m in others]
    got = [swap(value, "arc", m) for value, m in zip(sent, others)]
    x10 = send_x(x10)
    rhs = jnp.stack([pick(slices, arc)] + got)
    rhs, x10, x01, own[2], own[3] = together(rhs, x10, lead_rows(0, 1), own[2], own[3])
    far2, far3 = swap(own[2], "arc", 2), swap(own[3], "arc", 2)
    sent = rhs.astype(jnp.bfloat16)
    got = send_z([sent for _ in steps_out])
    x01 = send_x(x01)
    near = in_chunks(sent, got)
    split(1, 1, far1)
    kept0, sent0 = schur_parts(0, [x00, x10])
    near, sent0, x01, x11 = together(near, sent0, x01, lead_rows(1, 1))
    far = send_x(near)
    z0 = send_z(sent0)
    x11 = send_x(x11)
    own_damping = pick(pick(damping.reshape(pairs, 2, chunks, rows), side, 1).reshape(outers, rows), outer)
    damp = jnp.stack([own_damping] + [swap(own_damping, "arc", m) for m in others])
    split(2, 0, own[2])
    split(2, 1, far2)
    split(3, 0, own[3])
    split(3, 1, far3)
    kept1, sent1 = schur_parts(1, [x01, x11])
    far, z0, sent1, x02, x12 = together(far, z0, sent1, lead_rows(0, 2), lead_rows(1, 2))
    z1 = send_z(sent1)
    x02, x12 = send_x(x02), send_x(x12)
    ahead, own_part = through_columns(lead, rest, far, near)
    kept2, sent2 = schur_parts(2, [x02, x12])
    ahead, z1, sent2, x03 = together(ahead, z1, sent2, lead_rows(0, 3))
    got = send_x(ahead)
    z2 = send_z(sent2)
    x03 = send_x(x03)
    total = own_part + got
    total, z2, x03, x13 = together(total, z2, x03, lead_rows(1, 3))
    kept, sent = outer_parts(total)
    got = send_z(sent)
    x13 = send_x(x13)
    newton = rhs - damp[:, None, :] * add_all(kept, got)
    newton, x13 = together(newton.astype(jnp.bfloat16), x13)
    got = send_z([newton for _ in steps_out])
    near_y = in_chunks(newton, got)
    kept3, sent3 = schur_parts(3, [x03, x13])
    near_y, sent3 = together(near_y, sent3)
    far_y = send_x(near_y)
    z3 = send_z(sent3)
    demand_share = lax.dynamic_slice_in_dim(demands, arc * share, share, 2)
    steps = corrected_steps(lead, rest, far_y, near_y, lfactor, inverse, demand_share)
    schur_out = [add_all(kept, got) for kept, got in [(kept0, z0), (kept1, z1), (kept2, z2), (kept3, z3)]]

    def home(m):
        parts = [[jnp.where(side == which, near_y[n, m], far_y[n, m]) for n in range(chunks)] for which in range(2)]
        return jnp.concatenate([
            parts[which][n][:, j * rows : (j + 1) * rows]
            for j in range(pairs) for which in range(2) for n in range(chunks)], axis=1)
    held = jnp.stack([home(0)] + [swap(home(m), "arc", m) for m in others])
    newton_y = wide(jnp.concatenate([pick(held, arc ^ n) for n in range(arcs)])).T
    return (jnp.concatenate(schur_out, axis=0), newton_y, steps)


def solution(mesh):
    in_specs = (
        P("com", None, None),
        P("com", None, "arc"),
        P("com", "arc"),
        P("com", None, None),
        P("arc"),
    )
    out_specs = (P("com", "arc"), P("arc", None), P("com", None, "arc"))
    return jax.shard_map(
        on_device, mesh=mesh, in_specs=in_specs, out_specs=out_specs, check_vma=False
    )
```

```python
import functools
import jax, jax.numpy as jnp
from jax import lax
from jax.experimental import pallas as pl
from jax.experimental.pallas import tpu as pltpu
from jax.sharding import PartitionSpec as P

BLOCK = 128
LEAF = 16

def halves(value):
    high = value.astype(jnp.bfloat16)
    low = (value - high.astype(jnp.float32)).astype(jnp.bfloat16)
    return high, low

def dot(a, b):
    return jnp.dot(a, b, preferred_element_type=jnp.float32)

def dot3(a, b):
    return dot(a[0], b[0]) + (dot(a[0], b[1]) + dot(a[1], b[0]))

def tdot(a, b):
    return lax.dot_general(a, b, (((0,), (0,)), ((), ())), preferred_element_type=jnp.float32)

def leaf_inverses(packed):
    rows, lanes = packed.shape
    lane = lax.broadcasted_iota(jnp.int32, (rows, lanes), 1)
    row = lax.broadcasted_iota(jnp.int32, (rows, lanes), 0) % LEAF
    inverse = (lane % LEAF == row).astype(jnp.float32)
    groups = rows // LEAF
    first = lane // LEAF * LEAF
    for step in range(LEAF):
        column = jnp.take_along_axis(packed, first + step, axis=1, mode="promise_in_bounds")
        def at_step(a):
            picked = a.reshape(groups, LEAF, lanes)[:, step : step + 1, :]
            return jnp.broadcast_to(picked, (groups, LEAF, lanes)).reshape(rows, lanes)
        done = at_step(inverse) / at_step(column)
        inverse = jnp.where(row > step, inverse - column * done, jnp.where(row == step, done, inverse))
    return inverse

def block_inverses(blocks):
    size = BLOCK
    lane = lax.broadcasted_iota(jnp.int32, (LEAF, size), 1)
    def pack(block):
        out = jnp.zeros((LEAF, size), jnp.float32)
        for part in range(size // LEAF):
            out = jnp.where(lane // LEAF == part, block[part * LEAF : (part + 1) * LEAF, :], out)
        return out
    leaves = leaf_inverses(jnp.concatenate([pack(b) for b in blocks], axis=0))
    inverses = []
    for index in range(len(blocks)):
        leaf = leaves[index * LEAF : (index + 1) * LEAF]
        inverses.append(jnp.concatenate(
            [jnp.where(lane // LEAF == part, leaf, 0.0) for part in range(size // LEAF)], axis=0))
    width = LEAF
    while width < size:
        parts = [(p, p + width) for p in range(width, size, 2 * width)]
        out = []
        for block, inverse in zip(blocks, inverses):
            odd = jnp.concatenate([inverse[p:q] for p, q in parts], axis=0)
            low = []
            for p, q in parts:
                spot = lax.broadcasted_iota(jnp.int32, (width, size), 1)
                low.append(jnp.where((spot >= p - width) & (spot < p), block[p:q], 0.0))
            low = jnp.concatenate([jnp.concatenate([jnp.zeros_like(l), l], axis=0) for l in low], axis=0)
            term = dot3(halves(odd), halves(low))
            term = dot3(halves(term), halves(inverse))
            pieces = []
            for number, (p, q) in enumerate(parts):
                pieces += [inverse[p - width : p], inverse[p:q] - term[number * width : (number + 1) * width]]
            out.append(jnp.concatenate(pieces, axis=0))
        inverses = out
        width *= 2
    return inverses

def forward_kernel(side_ref, factor_ref, links_ref, usage_ref, demands_ref, out_ref, inverse_ref, rhs_ref, *others):
    *own_refs, both_ref, tail_ref = others
    coms, nodes, _ = factor_ref.shape
    count = nodes // BLOCK
    span = lambda i: slice(i * BLOCK, (i + 1) * BLOCK)

    @pl.when(pl.program_id(0) == 0)
    def _():
        blocks = [factor_ref[c, span(i), span(i)] for c in range(coms) for i in range(count)]
        inverses = block_inverses(blocks)
        for c in range(coms):
            for i in range(count):
                inverse_ref[c, span(i)] = inverses[c * count + i]
            for i in range(1, count):
                high, low = halves(factor_ref[c, span(i), : i * BLOCK])
                both_ref[c, i, :BLOCK, : i * BLOCK] = high
                both_ref[c, i, BLOCK:, : i * BLOCK] = low

    for i in range(count):
        for c in range(coms):
            mine = slice(c * nodes + i * BLOCK, c * nodes + (i + 1) * BLOCK)
            rest = links_ref[c, span(i)] * usage_ref[c].astype(jnp.float32)
            if i:
                before = slice(c * nodes, c * nodes + i * BLOCK)
                both = dot(both_ref[c, i, :, : i * BLOCK], out_ref[before])
                rest = rest - (both[:BLOCK] + (both[BLOCK:] + dot(both_ref[c, i, :BLOCK, : i * BLOCK], tail_ref[before])))
            high, low = halves(rest)
            inverse = halves(inverse_ref[c, span(i)])
            both = dot(jnp.concatenate(inverse, axis=0), high)
            high, low = halves(both[:BLOCK] + (both[BLOCK:] + dot(inverse[0], low)))
            out_ref[mine] = high
            tail_ref[mine] = low
    found = out_ref[...]
    rhs_ref[...] = tdot(demands_ref[...].reshape(coms * nodes, -1), found)
    for number, own_ref in enumerate(own_refs):
        width = own_ref.shape[1] // 2
        for which in range(2):
            start = pl.multiple_of((which ^ 1 ^ side_ref[0]) * (width * len(own_refs)) + number * width, width)
            own_ref[:, which * width : (which + 1) * width] = out_ref[:, pl.ds(start, width)]


def forward_solve(factor, links, usage, demands, side, chunks):
    coms, nodes, arcs = links.shape
    scens = demands.shape[2]
    tile = arcs
    span = arcs // 2 // chunks if chunks else 0
    depth = coms * nodes
    once = lambda *shape: pl.BlockSpec(shape, lambda t, _: (0,) * len(shape))
    return pl.pallas_call(
        forward_kernel,
        grid_spec=pltpu.PrefetchScalarGridSpec(
            num_scalar_prefetch=1,
            grid=(arcs // tile,),
            in_specs=[
                once(coms, nodes, nodes),
                pl.BlockSpec((coms, nodes, tile), lambda t, _: (0, 0, t)),
                pl.BlockSpec((coms, 1, tile), lambda t, _: (0, 0, t)),
                once(coms, nodes, scens),
            ],
            out_specs=[
                pl.BlockSpec((depth, tile), lambda t, _: (0, t)),
                once(coms, nodes, BLOCK),
                pl.BlockSpec((scens, tile), lambda t, _: (0, t)),
            ] + [once(depth, 2 * span)] * chunks,
            scratch_shapes=[
                pltpu.VMEM((coms, nodes // BLOCK, 2 * BLOCK, nodes), jnp.bfloat16),
                pltpu.VMEM((depth, tile), jnp.bfloat16),
            ],
        ),
        out_shape=[
            jax.ShapeDtypeStruct((depth, arcs), jnp.bfloat16),
            jax.ShapeDtypeStruct((coms, nodes, BLOCK), jnp.float32),
            jax.ShapeDtypeStruct((scens, arcs), jnp.float32),
        ] + [jax.ShapeDtypeStruct((depth, 2 * span), jnp.bfloat16)] * chunks,
        compiler_params=pltpu.CompilerParams(vmem_limit_bytes=48 * 2**20),
        cost_estimate=pl.CostEstimate(
            flops=6 * coms * nodes * nodes * arcs,
            bytes_accessed=4 * coms * nodes * (nodes + arcs) + 2 * coms * nodes * arcs, transcendentals=0),
    )(side.reshape(1), factor, links, usage.reshape(coms, 1, arcs), demands)


def backward_kernel(factor_ref, inverse_ref, demand_ref, correction_ref, out_ref):
    coms, nodes, _ = factor_ref.shape
    count = nodes // BLOCK
    span = lambda i: slice(i * BLOCK, (i + 1) * BLOCK)
    solved = [[] for _ in range(coms)]
    for i in reversed(range(count)):
        for c in range(coms):
            rest = demand_ref[c, span(i)].astype(jnp.float32).T - correction_ref[:, c * nodes + i * BLOCK : c * nodes + (i + 1) * BLOCK]
            if solved[c]:
                high = jnp.concatenate([h for h, _ in solved[c]], axis=1)
                low = jnp.concatenate([l for _, l in solved[c]], axis=1)
                rest = rest - dot3((high, low), halves(factor_ref[c, (i + 1) * BLOCK :, span(i)]))
            value = dot3(halves(rest), halves(inverse_ref[c, span(i)]))
            solved[c].insert(0, halves(value))
            out_ref[c, span(i)] = value.T

def multiply(pieces, value_ref):
    total = 0.0
    for (half, chunk), piece in pieces.items():
        value = jnp.concatenate([value_ref[chunk, 2 * half], value_ref[chunk, 2 * half + 1]], axis=1)
        total += lax.dot_general(value, piece[...], (((1,), (1,)), ((), ())), preferred_element_type=jnp.float32)
    return total


def inner_kernel(keys, *refs):
    count = len(keys)
    lead, rest = dict(zip(keys, refs[:count])), dict(zip(keys, refs[count : 2 * count]))
    far_ref, near_ref, lead_out, rest_out = refs[2 * count :]
    found = multiply(lead, far_ref) + multiply(rest, near_ref)
    scens = found.shape[0]
    both = jnp.concatenate(halves(found), axis=0)
    for pieces, out in ((lead, lead_out), (rest, rest_out)):
        for (half, chunk), piece in pieces.items():
            product = dot(both, piece[...])
            product = product[:scens] + product[scens:]
            span = product.shape[1] // 2
            out[chunk, 2 * half] = product[:, :span]
            out[chunk, 2 * half + 1] = product[:, span:]


def piece_cost(lead, times):
    pieces = len(lead) * 2
    depth, columns = next(iter(lead.values())).shape
    return dict(flops=2 * times * pieces * depth * columns * 64, bytes_accessed=2 * pieces * depth * columns, transcendentals=0)


def through_columns(lead, rest, far, near):
    keys = tuple(lead)
    shape = jax.ShapeDtypeStruct(far.shape, jnp.float32)
    return pl.pallas_call(
        functools.partial(inner_kernel, keys),
        out_shape=[shape, shape],
        compiler_params=pltpu.CompilerParams(vmem_limit_bytes=48 * 2**20),
        cost_estimate=pl.CostEstimate(**piece_cost(lead, 2)),
    )(*[lead[k] for k in keys], *[rest[k] for k in keys], far, near)


def steps_kernel(keys, *refs):
    count = len(keys)
    lead, rest = dict(zip(keys, refs[:count])), dict(zip(keys, refs[count : 2 * count]))
    far_ref, near_ref, factor_ref, inverse_ref, demand_ref, out_ref, correction_ref = refs[2 * count :]
    correction_ref[...] = multiply(rest, near_ref) + multiply(lead, far_ref)
    backward_kernel(factor_ref, inverse_ref, demand_ref, correction_ref, out_ref)


def corrected_steps(lead, rest, far, near, factor, inverse, demand):
    keys = tuple(lead)
    coms, nodes, scens = demand.shape
    return pl.pallas_call(
        functools.partial(steps_kernel, keys),
        out_shape=jax.ShapeDtypeStruct(demand.shape, jnp.float32),
        scratch_shapes=[pltpu.VMEM((scens, coms * nodes), jnp.float32)],
        compiler_params=pltpu.CompilerParams(vmem_limit_bytes=48 * 2**20),
        cost_estimate=pl.CostEstimate(**piece_cost(lead, 1)),
    )(*[lead[k] for k in keys], *[rest[k] for k in keys], far, near, factor, inverse, demand)


def bit_count(size):
    return size.bit_length() - 1


def swap(value, axis, bits):
    size = lax.axis_size(axis)
    return lax.ppermute(value, axis, [(i, i ^ bits) for i in range(size)])


def pick(value, index, dim=0):
    return lax.dynamic_index_in_dim(value, index, dim, keepdims=False)


def wide(value):
    return value.astype(jnp.float32)


def together(*values):
    return lax.optimization_barrier(values)


def on_device(lfactor, links, usage, demands, damping):
    place, arc = lax.axis_index("com"), lax.axis_index("arc")
    coms, arcs = lax.axis_size("com"), lax.axis_size("arc")
    side, outer, outers = place % 2, place // 2, coms // 2
    steps_out = range(1, outers)
    far_bits = [2 * step for step in steps_out]

    def send_x(value):
        return swap(value, "com", 1)

    def send_z(values):
        return [swap(value, "com", bits) for value, bits in zip(values, far_bits)]

    count, nodes, width = links.shape
    depth = count * nodes
    scens = demands.shape[2]
    share = scens // arcs
    chunks = arcs
    pairs = outers // chunks
    rows = width // coms
    span = pairs * rows
    direct = pairs == 1 and rows % 128 == 0
    panel, inverse, local, *own = forward_solve(lfactor, links, usage, demands, side, chunks if direct else 0)
    halves_of = range(arcs // 2)

    def columns_of(value, which, chunk):
        starts = [((j * 2 + which) * chunks + chunk) * rows for j in range(pairs)]
        parts = [lax.dynamic_slice_in_dim(value, start, rows, value.ndim - 1) for start in starts]
        return jnp.concatenate(parts, axis=-1)

    if not direct:
        own = [jnp.concatenate([columns_of(panel, 1 - side, n), columns_of(panel, side, n)], axis=1) for n in range(chunks)]
    lead, rest = {}, {}

    def split(chunk, half, first):
        second = swap(first, "arc", 1)
        lead[half, chunk] = jnp.concatenate([first[:, :span], second[:, :span]], axis=1)
        rest[half, chunk] = jnp.concatenate([first[:, span:], second[:, span:]], axis=1)

    def lead_rows(half, chunk):
        return tdot(lead[half, chunk], panel).astype(jnp.bfloat16)

    def schur_parts(chunk, got):
        total = jnp.concatenate([tdot(rest[h, chunk], panel) + wide(got[h]) for h in halves_of])
        total = total.reshape(arcs, pairs, rows, width)
        def block_for(step):
            to = outer ^ step
            return pick(pick(total, arc ^ (to // pairs)), to % pairs)
        return block_for(0), [block_for(step).astype(jnp.bfloat16) for step in steps_out]

    def add_all(kept, got):
        return sum((wide(g) for g in got), kept)

    def outer_parts(total):
        def part(owner):
            return lax.dynamic_slice_in_dim(pick(total, owner % chunks), owner // chunks * rows, rows, total.ndim - 2)
        return part(outer), [part(outer ^ step) for step in steps_out]

    def in_chunks(value, got):
        held = jnp.stack([value] + got)
        owners = [pick(held, outer ^ n) for n in range(outers)]
        return jnp.stack([jnp.concatenate(owners[n::chunks], axis=-1) for n in range(chunks)])

    def of_side(which):
        return jnp.stack([columns_of(local, which, n) for n in range(chunks)])
    others = range(1, arcs)
    got = send_x(of_side(1 - side))
    far0 = swap(own[0], "arc", 2)
    split(0, 0, own[0])
    split(1, 0, own[1])
    total = of_side(side) + got
    total, x00, own[1] = together(total, lead_rows(0, 0), own[1])
    kept, sent = outer_parts(total)
    far1 = swap(own[1], "arc", 2)
    got = send_z(sent)
    x00 = send_x(x00)
    split(0, 1, far0)
    own_rhs = add_all(kept, got)
    own_rhs, x00, x10 = together(own_rhs, x00, lead_rows(1, 0))
    slices = own_rhs.reshape(arcs, share, rows)
    sent = [pick(slices, arc ^ m) for m in others]
    got = [swap(value, "arc", m) for value, m in zip(sent, others)]
    x10 = send_x(x10)
    rhs = jnp.stack([pick(slices, arc)] + got)
    rhs, x10, x01, own[2], own[3] = together(rhs, x10, lead_rows(0, 1), own[2], own[3])
    far2, far3 = swap(own[2], "arc", 2), swap(own[3], "arc", 2)
    sent = rhs.astype(jnp.bfloat16)
    got = send_z([sent for _ in steps_out])
    x01 = send_x(x01)
    near = in_chunks(sent, got)
    split(1, 1, far1)
    kept0, sent0 = schur_parts(0, [x00, x10])
    near, sent0, x01, x11 = together(near, sent0, x01, lead_rows(1, 1))
    far = send_x(near)
    z0 = send_z(sent0)
    x11 = send_x(x11)
    own_damping = pick(pick(damping.reshape(pairs, 2, chunks, rows), side, 1).reshape(outers, rows), outer)
    damp = jnp.stack([own_damping] + [swap(own_damping, "arc", m) for m in others])
    split(2, 0, own[2])
    split(2, 1, far2)
    split(3, 0, own[3])
    split(3, 1, far3)
    kept1, sent1 = schur_parts(1, [x01, x11])
    far, z0, sent1, x02, x12 = together(far, z0, sent1, lead_rows(0, 2), lead_rows(1, 2))
    z1 = send_z(sent1)
    x02, x12 = send_x(x02), send_x(x12)
    ahead, own_part = through_columns(lead, rest, far, near)
    kept2, sent2 = schur_parts(2, [x02, x12])
    ahead, z1, sent2, x03 = together(ahead, z1, sent2, lead_rows(0, 3))
    got = send_x(ahead)
    z2 = send_z(sent2)
    x03 = send_x(x03)
    total = own_part + got
    total, z2, x03, x13 = together(total, z2, x03, lead_rows(1, 3))
    kept, sent = outer_parts(total)
    got = send_z(sent)
    x13 = send_x(x13)
    newton = rhs - damp[:, None, :] * add_all(kept, got)
    newton, x13 = together(newton.astype(jnp.bfloat16), x13)
    got = send_z([newton for _ in steps_out])
    near_y = in_chunks(newton, got)
    kept3, sent3 = schur_parts(3, [x03, x13])
    near_y, sent3 = together(near_y, sent3)
    far_y = send_x(near_y)
    z3 = send_z(sent3)
    demand_share = lax.dynamic_slice_in_dim(demands, arc * share, share, 2)
    steps = corrected_steps(lead, rest, far_y, near_y, lfactor, inverse, demand_share)
    schur_out = [add_all(kept, got) for kept, got in [(kept0, z0), (kept1, z1), (kept2, z2), (kept3, z3)]]

    def home(m):
        parts = [[jnp.where(side == which, near_y[n, m], far_y[n, m]) for n in range(chunks)] for which in range(2)]
        return jnp.concatenate([
            parts[which][n][:, j * rows : (j + 1) * rows]
            for j in range(pairs) for which in range(2) for n in range(chunks)], axis=1)
    held = jnp.stack([home(0)] + [swap(home(m), "arc", m) for m in others])
    newton_y = wide(jnp.concatenate([pick(held, arc ^ n) for n in range(arcs)])).T
    return (jnp.concatenate(schur_out, axis=0), newton_y, steps)


def solution(mesh):
    in_specs = (
        P("com", None, None),
        P("com", None, "arc"),
        P("com", "arc"),
        P("com", None, None),
        P("arc"),
    )
    out_specs = (P("com", "arc"), P("arc", None), P("com", None, "arc"))
    return jax.shard_map(
        on_device, mesh=mesh, in_specs=in_specs, out_specs=out_specs, check_vma=False
    )
```

```python
import functools
import jax, jax.numpy as jnp
from jax import lax
from jax.experimental import pallas as pl
from jax.experimental.pallas import tpu as pltpu
from jax.sharding import PartitionSpec as P

BLOCK = 128
LEAF = 16

def halves(value):
    high = value.astype(jnp.bfloat16)
    low = (value - high.astype(jnp.float32)).astype(jnp.bfloat16)
    return high, low

def dot(a, b):
    return jnp.dot(a, b, preferred_element_type=jnp.float32)

def dot3(a, b):
    return dot(a[0], b[0]) + (dot(a[0], b[1]) + dot(a[1], b[0]))

def tdot(a, b):
    return lax.dot_general(a, b, (((0,), (0,)), ((), ())), preferred_element_type=jnp.float32)

def leaf_inverses(packed):
    rows, lanes = packed.shape
    lane = lax.broadcasted_iota(jnp.int32, (rows, lanes), 1)
    row = lax.broadcasted_iota(jnp.int32, (rows, lanes), 0) % LEAF
    inverse = (lane % LEAF == row).astype(jnp.float32)
    groups = rows // LEAF
    first = lane // LEAF * LEAF
    for step in range(LEAF):
        column = jnp.take_along_axis(packed, first + step, axis=1, mode="promise_in_bounds")
        def at_step(a):
            picked = a.reshape(groups, LEAF, lanes)[:, step : step + 1, :]
            return jnp.broadcast_to(picked, (groups, LEAF, lanes)).reshape(rows, lanes)
        done = at_step(inverse) / at_step(column)
        inverse = jnp.where(row > step, inverse - column * done, jnp.where(row == step, done, inverse))
    return inverse

def block_inverses(blocks):
    size = BLOCK
    lane = lax.broadcasted_iota(jnp.int32, (LEAF, size), 1)
    def pack(block):
        out = jnp.zeros((LEAF, size), jnp.float32)
        for part in range(size // LEAF):
            out = jnp.where(lane // LEAF == part, block[part * LEAF : (part + 1) * LEAF, :], out)
        return out
    leaves = leaf_inverses(jnp.concatenate([pack(b) for b in blocks], axis=0))
    inverses = []
    for index in range(len(blocks)):
        leaf = leaves[index * LEAF : (index + 1) * LEAF]
        inverses.append(jnp.concatenate(
            [jnp.where(lane // LEAF == part, leaf, 0.0) for part in range(size // LEAF)], axis=0))
    width = LEAF
    while width < size:
        parts = [(p, p + width) for p in range(width, size, 2 * width)]
        out = []
        for block, inverse in zip(blocks, inverses):
            odd = jnp.concatenate([inverse[p:q] for p, q in parts], axis=0)
            low = []
            for p, q in parts:
                spot = lax.broadcasted_iota(jnp.int32, (width, size), 1)
                low.append(jnp.where((spot >= p - width) & (spot < p), block[p:q], 0.0))
            low = jnp.concatenate([jnp.concatenate([jnp.zeros_like(l), l], axis=0) for l in low], axis=0)
            term = dot3(halves(odd), halves(low))
            term = dot3(halves(term), halves(inverse))
            pieces = []
            for number, (p, q) in enumerate(parts):
                pieces += [inverse[p - width : p], inverse[p:q] - term[number * width : (number + 1) * width]]
            out.append(jnp.concatenate(pieces, axis=0))
        inverses = out
        width *= 2
    return inverses

def forward_kernel(side_ref, factor_ref, links_ref, usage_ref, demands_ref, out_ref, inverse_ref, rhs_ref, *others):
    *own_refs, high_ref, low_ref = others
    coms, nodes, _ = factor_ref.shape
    count = nodes // BLOCK
    span = lambda i: slice(i * BLOCK, (i + 1) * BLOCK)

    @pl.when(pl.program_id(0) == 0)
    def _():
        blocks = [factor_ref[c, span(i), span(i)] for c in range(coms) for i in range(count)]
        inverses = block_inverses(blocks)
        for c in range(coms):
            for i in range(count):
                inverse_ref[c, span(i)] = inverses[c * count + i]
            high, low = halves(factor_ref[c])
            high_ref[c] = high
            low_ref[c] = low

    solved = [[] for _ in range(coms)]
    for i in range(count):
        for c in range(coms):
            rest = links_ref[c, span(i)] * usage_ref[c].astype(jnp.float32)
            if i:
                high = jnp.concatenate([h for h, _ in solved[c]], axis=0)
                low = jnp.concatenate([l for _, l in solved[c]], axis=0)
                rest = rest - dot3((high_ref[c, span(i), : i * BLOCK], low_ref[c, span(i), : i * BLOCK]), (high, low))
            value = dot3(halves(inverse_ref[c, span(i)]), halves(rest))
            solved[c].append(halves(value))
            out_ref[c * nodes + i * BLOCK : c * nodes + (i + 1) * BLOCK] = solved[c][-1][0]
    found = jnp.concatenate([h for c in range(coms) for h, _ in solved[c]], axis=0)
    rhs_ref[...] = tdot(demands_ref[...].reshape(coms * nodes, -1), found)
    if own_refs:
        width = found.shape[1] // len(own_refs)
        spot = pl.ds(pl.multiple_of(jnp.where(pl.program_id(0) == side_ref[0], width, 0), width), width)
        for number, own_ref in enumerate(own_refs):
            own_ref[:, spot] = found[:, number * width : (number + 1) * width]

def forward_solve(factor, links, usage, demands, side, chunks):
    coms, nodes, arcs = links.shape
    scens = demands.shape[2]
    tile = arcs // 2
    span = tile // chunks if chunks else 0
    depth = coms * nodes
    once = lambda *shape: pl.BlockSpec(shape, lambda t, _: (0,) * len(shape))
    return pl.pallas_call(
        forward_kernel,
        grid_spec=pltpu.PrefetchScalarGridSpec(
            num_scalar_prefetch=1,
            grid=(arcs // tile,),
            in_specs=[
                once(coms, nodes, nodes),
                pl.BlockSpec((coms, nodes, tile), lambda t, _: (0, 0, t)),
                pl.BlockSpec((coms, 1, tile), lambda t, _: (0, 0, t)),
                once(coms, nodes, scens),
            ],
            out_specs=[
                pl.BlockSpec((depth, tile), lambda t, _: (0, t)),
                once(coms, nodes, BLOCK),
                pl.BlockSpec((scens, tile), lambda t, _: (0, t)),
            ] + [once(depth, 2 * span)] * chunks,
            scratch_shapes=[pltpu.VMEM((coms, nodes, nodes), jnp.bfloat16)] * 2,
        ),
        out_shape=[
            jax.ShapeDtypeStruct((depth, arcs), jnp.bfloat16),
            jax.ShapeDtypeStruct((coms, nodes, BLOCK), jnp.float32),
            jax.ShapeDtypeStruct((scens, arcs), jnp.float32),
        ] + [jax.ShapeDtypeStruct((depth, 2 * span), jnp.bfloat16)] * chunks,
        compiler_params=pltpu.CompilerParams(vmem_limit_bytes=48 * 2**20),
        cost_estimate=pl.CostEstimate(
            flops=6 * coms * nodes * nodes * arcs,
            bytes_accessed=4 * coms * nodes * (nodes + arcs) + 2 * coms * nodes * arcs, transcendentals=0),
    )(side.reshape(1), factor, links, usage.reshape(coms, 1, arcs), demands)


def backward_kernel(factor_ref, inverse_ref, demand_ref, correction_ref, out_ref):
    coms, nodes, _ = factor_ref.shape
    count = nodes // BLOCK
    span = lambda i: slice(i * BLOCK, (i + 1) * BLOCK)
    solved = [[] for _ in range(coms)]
    for i in reversed(range(count)):
        for c in range(coms):
            rest = demand_ref[c, span(i)].astype(jnp.float32).T - correction_ref[:, c * nodes + i * BLOCK : c * nodes + (i + 1) * BLOCK]
            if solved[c]:
                high = jnp.concatenate([h for h, _ in solved[c]], axis=1)
                low = jnp.concatenate([l for _, l in solved[c]], axis=1)
                rest = rest - dot3((high, low), halves(factor_ref[c, (i + 1) * BLOCK :, span(i)]))
            value = dot3(halves(rest), halves(inverse_ref[c, span(i)]))
            solved[c].insert(0, halves(value))
            out_ref[c, span(i)] = value.T

def multiply(pieces, value_ref):
    total = 0.0
    for (half, chunk), piece in pieces.items():
        value = jnp.concatenate([value_ref[chunk, 2 * half], value_ref[chunk, 2 * half + 1]], axis=1)
        total += lax.dot_general(value, piece[...], (((1,), (1,)), ((), ())), preferred_element_type=jnp.float32)
    return total


def inner_kernel(keys, *refs):
    count = len(keys)
    lead, rest = dict(zip(keys, refs[:count])), dict(zip(keys, refs[count : 2 * count]))
    far_ref, near_ref, lead_out, rest_out = refs[2 * count :]
    found = multiply(lead, far_ref) + multiply(rest, near_ref)
    scens = found.shape[0]
    both = jnp.concatenate(halves(found), axis=0)
    for pieces, out in ((lead, lead_out), (rest, rest_out)):
        for (half, chunk), piece in pieces.items():
            product = dot(both, piece[...])
            product = product[:scens] + product[scens:]
            span = product.shape[1] // 2
            out[chunk, 2 * half] = product[:, :span]
            out[chunk, 2 * half + 1] = product[:, span:]


def piece_cost(lead, times):
    pieces = len(lead) * 2
    depth, columns = next(iter(lead.values())).shape
    return dict(flops=2 * times * pieces * depth * columns * 64, bytes_accessed=2 * pieces * depth * columns, transcendentals=0)


def through_columns(lead, rest, far, near):
    keys = tuple(lead)
    shape = jax.ShapeDtypeStruct(far.shape, jnp.float32)
    return pl.pallas_call(
        functools.partial(inner_kernel, keys),
        out_shape=[shape, shape],
        compiler_params=pltpu.CompilerParams(vmem_limit_bytes=48 * 2**20),
        cost_estimate=pl.CostEstimate(**piece_cost(lead, 2)),
    )(*[lead[k] for k in keys], *[rest[k] for k in keys], far, near)


def steps_kernel(keys, *refs):
    count = len(keys)
    lead, rest = dict(zip(keys, refs[:count])), dict(zip(keys, refs[count : 2 * count]))
    far_ref, near_ref, factor_ref, inverse_ref, demand_ref, out_ref, correction_ref = refs[2 * count :]
    correction_ref[...] = multiply(rest, near_ref) + multiply(lead, far_ref)
    backward_kernel(factor_ref, inverse_ref, demand_ref, correction_ref, out_ref)


def corrected_steps(lead, rest, far, near, factor, inverse, demand):
    keys = tuple(lead)
    coms, nodes, scens = demand.shape
    return pl.pallas_call(
        functools.partial(steps_kernel, keys),
        out_shape=jax.ShapeDtypeStruct(demand.shape, jnp.float32),
        scratch_shapes=[pltpu.VMEM((scens, coms * nodes), jnp.float32)],
        compiler_params=pltpu.CompilerParams(vmem_limit_bytes=48 * 2**20),
        cost_estimate=pl.CostEstimate(**piece_cost(lead, 1)),
    )(*[lead[k] for k in keys], *[rest[k] for k in keys], far, near, factor, inverse, demand)


def bit_count(size):
    return size.bit_length() - 1


def swap(value, axis, bits):
    size = lax.axis_size(axis)
    return lax.ppermute(value, axis, [(i, i ^ bits) for i in range(size)])


def pick(value, index, dim=0):
    return lax.dynamic_index_in_dim(value, index, dim, keepdims=False)


def wide(value):
    return value.astype(jnp.float32)


def together(*values):
    return lax.optimization_barrier(values)


def on_device(lfactor, links, usage, demands, damping):
    place, arc = lax.axis_index("com"), lax.axis_index("arc")
    coms, arcs = lax.axis_size("com"), lax.axis_size("arc")
    side, outer, outers = place % 2, place // 2, coms // 2
    steps_out = range(1, outers)
    far_bits = [2 * step for step in steps_out]

    def send_x(value):
        return swap(value, "com", 1)

    def send_z(values):
        return [swap(value, "com", bits) for value, bits in zip(values, far_bits)]

    count, nodes, width = links.shape
    depth = count * nodes
    scens = demands.shape[2]
    share = scens // arcs
    chunks = arcs
    pairs = outers // chunks
    rows = width // coms
    span = pairs * rows
    direct = pairs == 1 and rows % 128 == 0
    panel, inverse, local, *own = forward_solve(lfactor, links, usage, demands, side, chunks if direct else 0)
    halves_of = range(arcs // 2)

    def columns_of(value, which, chunk):
        starts = [((j * 2 + which) * chunks + chunk) * rows for j in range(pairs)]
        parts = [lax.dynamic_slice_in_dim(value, start, rows, value.ndim - 1) for start in starts]
        return jnp.concatenate(parts, axis=-1)

    if not direct:
        own = [jnp.concatenate([columns_of(panel, 1 - side, n), columns_of(panel, side, n)], axis=1) for n in range(chunks)]
    lead, rest = {}, {}

    def split(chunk, half, first):
        second = swap(first, "arc", 1)
        lead[half, chunk] = jnp.concatenate([first[:, :span], second[:, :span]], axis=1)
        rest[half, chunk] = jnp.concatenate([first[:, span:], second[:, span:]], axis=1)

    def lead_rows(half, chunk):
        return tdot(lead[half, chunk], panel).astype(jnp.bfloat16)

    def schur_parts(chunk, got):
        total = jnp.concatenate([tdot(rest[h, chunk], panel) + wide(got[h]) for h in halves_of])
        total = total.reshape(arcs, pairs, rows, width)
        def block_for(step):
            to = outer ^ step
            return pick(pick(total, arc ^ (to // pairs)), to % pairs)
        return block_for(0), [block_for(step).astype(jnp.bfloat16) for step in steps_out]

    def add_all(kept, got):
        return sum((wide(g) for g in got), kept)

    def outer_parts(total):
        def part(owner):
            return lax.dynamic_slice_in_dim(pick(total, owner % chunks), owner // chunks * rows, rows, total.ndim - 2)
        return part(outer), [part(outer ^ step) for step in steps_out]

    def in_chunks(value, got):
        held = jnp.stack([value] + got)
        owners = [pick(held, outer ^ n) for n in range(outers)]
        return jnp.stack([jnp.concatenate(owners[n::chunks], axis=-1) for n in range(chunks)])

    def of_side(which):
        return jnp.stack([columns_of(local, which, n) for n in range(chunks)])
    others = range(1, arcs)
    got = send_x(of_side(1 - side))
    far0 = swap(own[0], "arc", 2)
    split(0, 0, own[0])
    split(1, 0, own[1])
    total = of_side(side) + got
    total, x00, own[1] = together(total, lead_rows(0, 0), own[1])
    kept, sent = outer_parts(total)
    far1 = swap(own[1], "arc", 2)
    got = send_z(sent)
    x00 = send_x(x00)
    split(0, 1, far0)
    own_rhs = add_all(kept, got)
    own_rhs, x00, x10 = together(own_rhs, x00, lead_rows(1, 0))
    slices = own_rhs.reshape(arcs, share, rows)
    sent = [pick(slices, arc ^ m) for m in others]
    got = [swap(value, "arc", m) for value, m in zip(sent, others)]
    x10 = send_x(x10)
    rhs = jnp.stack([pick(slices, arc)] + got)
    rhs, x10, x01, own[2], own[3] = together(rhs, x10, lead_rows(0, 1), own[2], own[3])
    far2, far3 = swap(own[2], "arc", 2), swap(own[3], "arc", 2)
    sent = rhs.astype(jnp.bfloat16)
    got = send_z([sent for _ in steps_out])
    x01 = send_x(x01)
    near = in_chunks(sent, got)
    split(1, 1, far1)
    kept0, sent0 = schur_parts(0, [x00, x10])
    near, sent0, x01, x11 = together(near, sent0, x01, lead_rows(1, 1))
    far = send_x(near)
    z0 = send_z(sent0)
    x11 = send_x(x11)
    own_damping = pick(pick(damping.reshape(pairs, 2, chunks, rows), side, 1).reshape(outers, rows), outer)
    damp = jnp.stack([own_damping] + [swap(own_damping, "arc", m) for m in others])
    split(2, 0, own[2])
    split(2, 1, far2)
    split(3, 0, own[3])
    split(3, 1, far3)
    kept1, sent1 = schur_parts(1, [x01, x11])
    far, z0, sent1, x02, x12 = together(far, z0, sent1, lead_rows(0, 2), lead_rows(1, 2))
    z1 = send_z(sent1)
    x02, x12 = send_x(x02), send_x(x12)
    ahead, own_part = through_columns(lead, rest, far, near)
    kept2, sent2 = schur_parts(2, [x02, x12])
    ahead, z1, sent2, x03 = together(ahead, z1, sent2, lead_rows(0, 3))
    got = send_x(ahead)
    z2 = send_z(sent2)
    x03 = send_x(x03)
    total = own_part + got
    total, z2, x13 = together(total, z2, lead_rows(1, 3))
    kept, sent = outer_parts(total)
    got = send_z(sent)
    x13 = send_x(x13)
    newton = rhs - damp[:, None, :] * add_all(kept, got)
    newton, x13 = together(newton.astype(jnp.bfloat16), x13)
    got = send_z([newton for _ in steps_out])
    near_y = in_chunks(newton, got)
    kept3, sent3 = schur_parts(3, [x03, x13])
    near_y, sent3 = together(near_y, sent3)
    far_y = send_x(near_y)
    z3 = send_z(sent3)
    demand_share = lax.dynamic_slice_in_dim(demands, arc * share, share, 2)
    steps = corrected_steps(lead, rest, far_y, near_y, lfactor, inverse, demand_share)
    schur_out = [add_all(kept, got) for kept, got in [(kept0, z0), (kept1, z1), (kept2, z2), (kept3, z3)]]

    def home(m):
        parts = [[jnp.where(side == which, near_y[n, m], far_y[n, m]) for n in range(chunks)] for which in range(2)]
        return jnp.concatenate([
            parts[which][n][:, j * rows : (j + 1) * rows]
            for j in range(pairs) for which in range(2) for n in range(chunks)], axis=1)
    held = jnp.stack([home(0)] + [swap(home(m), "arc", m) for m in others])
    newton_y = wide(jnp.concatenate([pick(held, arc ^ n) for n in range(arcs)])).T
    return (jnp.concatenate(schur_out, axis=0), newton_y, steps)


def solution(mesh):
    in_specs = (
        P("com", None, None),
        P("com", None, "arc"),
        P("com", "arc"),
        P("com", None, None),
        P("arc"),
    )
    out_specs = (P("com", "arc"), P("arc", None), P("com", None, "arc"))
    return jax.shard_map(
        on_device, mesh=mesh, in_specs=in_specs, out_specs=out_specs, check_vma=False
    )
```
